32 devices in a mesh: group: 2 (over x), run: 2 (over core), shard: 8 (over z, y).
Axes of the slice: x: 2, y: 2, z: 4, core: 2. Of those that a mesh axis runs over, the one named last changes fastest.
Arguments:
- weight: float32 [8, 4096, 512], P(('group', 'run'), 'shard'), parts along dimension 0, may hold values from -6 to 6
- first_moment: float32 [8, 4096, 512], P(('group', 'run'), 'shard'), parts along dimension 0, may hold values from -6 to 6
- second_moment: float32 [8, 4096, 512], P(('group', 'run'), 'shard'), parts along dimension 0, may hold values from 0.5 to 4
- norm_gain: float32 [8, 4096], P(('group', 'run')), parts along dimension 0, may hold values from 0.25 to 1.75
- learning_rate: float32 [8], P(('group', 'run')), parts along dimension 0, may hold values from 0.05 to 0.3
- momentum: float32 [8], P(('group', 'run')), parts along dimension 0, may hold values from 0.8 to 0.95
- inputs: bfloat16 [8, 6144, 4096], P(('group', 'run'), 'shard'), parts along dimension 0, may hold values from -6 to 6
- cotangent: bfloat16 [8, 6144, 512], P(('group', 'run'), 'shard'), parts along dimension 0, may hold values from -6 to 6
- winner: int32 [8], P('group'), parts along dimension 0, may hold values from 0 to 3, as said below
- perturb: int32 [8, 2], P('group'), parts along dimension 0, may hold values from 0 to 1
Outputs:
- keys: bfloat16 [8, 6144, 512], P(('group', 'run'), 'shard'), parts along dimension 0
- new_weight: float32 [8, 4096, 512], P(('group', 'run'), 'shard'), parts along dimension 0
- new_first: float32 [8, 4096, 512], P(('group', 'run'), 'shard'), parts along dimension 0
- new_second: float32 [8, 4096, 512], P(('group', 'run'), 'shard'), parts along dimension 0
- new_hyper: float32 [8, 2], P(('group', 'run')), parts along dimension 0
The draws below stay inside these ranges and needn't reach their ends.
There are 2 independent parts, one for each index of `group`. The reference program is written for one: setup_inputs(seed, part) draws one part's arguments, and reference() takes and returns one part's arrays. A program takes and returns all parts, laid end to end along the dimension named above; each array names one. Nothing has to cross between parts.
Inputs may be any that keep to these rules, and one draw needn't show every extreme that they name: `winner`: 2 runs name themselves; every other run names one of those.
All inputs are finite; a program needn't handle non-finite values.
Results may differ from the reference program's by a relative error of at most 0.0058.
Values may be sent and summed in bfloat16 or wider, within the bound.
A program may use at most 192 MiB of HBM per device.

```python
import math
import jax
import jax.numpy as jnp
from jax import lax

D = 4096
KW = 512
RUNS = 4
TOKENS = 6144


def draw_winner(key, part):
    key = jax.random.fold_in(key, 7)
    order_key, pick_key = jax.random.split(key)
    order = jax.random.permutation(order_key, RUNS).astype(jnp.int32)
    keepers = RUNS // 2
    winners = order[:keepers]
    losers = order[keepers:]
    picks = jax.random.randint(pick_key, (RUNS - keepers,), 0, keepers)
    result = jnp.arange(RUNS, dtype=jnp.int32)
    return result.at[losers].set(winners[picks]).astype(jnp.int32)


def touch_ends(entries, stream_key, low, largest):
    extent = entries.shape
    spot = [jax.random.randint(jax.random.fold_in(stream_key, axis), (), 0, extent[axis]) for axis in range(len(extent))]
    entries = entries.at[tuple(spot)].set(low)
    longest = extent.index(max(extent))
    spot[longest] = (spot[longest] + 1) % extent[longest]
    return entries.at[tuple(spot)].set(largest)


def shard_levels(stream_key, extent, shards, low, top_value):
    factor_of = 1.0
    for dim, parts in shards:
        steps = jax.random.uniform(jax.random.fold_in(jax.random.fold_in(stream_key, 6), dim), (parts,), jnp.float32, low / len(shards), top_value / len(shards))
        factor_of = factor_of * jnp.repeat(jnp.exp(steps), extent[dim] // parts).reshape((-1,) + (1,) * (len(extent) - 1 - dim))
    return factor_of


def noise(own_key, dims, width, reach, cuts=(), kind=jnp.bfloat16):
    entries = width * jax.random.normal(own_key, dims, jnp.float32)
    if cuts:
        entries = entries * shard_levels(own_key, dims, cuts, -0.22, 0.18)
    return jnp.clip(entries, -reach, reach).astype(kind)


def setup_inputs(seed: int = 0, part: int = 0) -> dict:
    splits = jax.random.split(jax.random.key(seed), 11)
    part_keys = jax.random.split(jax.random.fold_in(splits[10], part), 11)
    return {
        "weight": noise(part_keys[0], (RUNS, D, KW), 1.0, 6.0, ((0, 2), (1, 8)), jnp.float32),
        "first_moment": noise(part_keys[1], (RUNS, D, KW), 1.0, 6.0, ((0, 2), (1, 8)), jnp.float32),
        "second_moment": jnp.clip(jnp.exp(math.log(4.0) - 2.0794415 * jax.random.uniform(part_keys[2], (RUNS, D, KW), jnp.float32) ** shard_levels(part_keys[2], (RUNS, D, KW), ((0, 2), (1, 8)), -0.2, 0.2)), 0.5, 4.0),
        "norm_gain": jnp.clip(1.0 + 0.15 * jax.random.normal(part_keys[3], (RUNS, D), jnp.float32), 0.25, 1.75),
        "learning_rate": jnp.clip(jnp.exp(math.log(0.3) - 1.7917595 * jax.random.uniform(part_keys[4], (RUNS,), jnp.float32) ** shard_levels(part_keys[4], (RUNS,), ((0, 2),), -0.2, 0.2)), 0.05, 0.3),
        "momentum": jnp.clip(0.8 + 0.14999998 * jax.random.uniform(part_keys[5], (RUNS,), jnp.float32) ** shard_levels(part_keys[5], (RUNS,), ((0, 2),), -0.2, 0.2), 0.8, 0.95),
        "inputs": noise(part_keys[6], (RUNS, TOKENS, D), 1.0, 6.0, ((0, 2), (1, 8))),
        "cotangent": noise(part_keys[7], (RUNS, TOKENS, KW), 1.0, 6.0, ((0, 2), (1, 8))),
        "winner": draw_winner(jax.random.fold_in(jax.random.fold_in(splits[10], part), 71), part),
        "perturb": touch_ends(jax.random.randint(part_keys[9], (RUNS, 2), 0, 2), jax.random.fold_in(part_keys[9], 1), 0, 1).astype(jnp.int32),
    }


def reference(weight, first_moment, second_moment, norm_gain, learning_rate, momentum, inputs, cotangent, winner, perturb):
    runs_iota = jnp.arange(RUNS, dtype=jnp.int32)
    loser = winner != runs_iota
    taken_weight = jnp.take(weight, winner, axis=0)
    taken_first = jnp.take(first_moment, winner, axis=0)
    taken_second = jnp.take(second_moment, winner, axis=0)
    taken_gain = jnp.take(norm_gain, winner, axis=0)
    taken_rate = jnp.take(learning_rate, winner, axis=0)
    taken_momentum = jnp.take(momentum, winner, axis=0)
    factor = jnp.where(perturb == 0, jnp.float32(0.8), jnp.float32(1.25))
    factor = jnp.where(loser[:, None], factor, jnp.float32(1.0))
    rate = taken_rate * factor[:, 0]
    beta = 1.0 - (1.0 - taken_momentum) * factor[:, 1]
    new_hyper = jnp.stack([rate, beta], axis=1)
    scale = D ** (-0.5)
    keys_list = []
    grad_list = []
    for index in range(RUNS):
        values = inputs[index].astype(jnp.float32)
        square = lax.optimization_barrier(jnp.mean(values * values, axis=-1, keepdims=True))
        normed = (values * lax.rsqrt(square + 1e-05) * taken_gain[index][None, :]).astype(jnp.bfloat16)
        wide = taken_weight[index].astype(jnp.bfloat16)
        keys_list.append((jnp.dot(normed, wide, preferred_element_type=jnp.float32) * scale).astype(jnp.bfloat16))
        grad_list.append(jnp.dot(normed.T, cotangent[index], preferred_element_type=jnp.float32) * scale)
    keys = jnp.stack(keys_list)
    grad = jnp.stack(grad_list)
    beta_full = beta[:, None, None]
    new_first = beta_full * taken_first + (1.0 - beta_full) * grad
    new_second = 0.95 * taken_second + 0.05 * grad * grad
    new_weight = taken_weight - rate[:, None, None] * new_first / (jnp.sqrt(new_second) + 1e-08)
    return (keys, new_weight, new_first, new_second, new_hyper)
```

```python
import functools

import jax
import jax.numpy as jnp
from jax import lax
from jax.experimental import pallas as pl
from jax.experimental.pallas import tpu as pltpu
from jax.sharding import PartitionSpec as P

MESH = pl.DeviceIdType.MESH
F32 = jnp.float32
BF16 = jnp.bfloat16
AHEAD = 3


def visit_order(planes):
    return [sorted(range(planes), key=lambda d: (-abs(d - z), -d)) for z in range(planes)]


def exchange_kernel(
    n,
    pick_ref,
    mine_ref,
    x_hbm,
    cot_hbm,
    w_hbm,
    f_hbm,
    s_hbm,
    side_hbm,
    keys_hbm,
    grad_hbm,
    w_out,
    f_out,
    s_out,
    side_out,
    x,
    cot,
    inv,
    w4,
    side4,
    ysend,
    yrecv,
    zrecv,
    gmine,
    gother,
    acc,
    tmp,
    in_sem,
    own_sem,
    out_sem,
    st_send,
    st_recv,
    y_send,
    y_recv,
    z_send,
    z_recv,
    ay_send,
    up_send,
    dn_send,
    ag_recv,
    co_send,
    co_recv,
):
    planes = n // 2
    steps = 2 * planes
    runs, tokens, features = x.shape
    rows = features // n
    width = cot.shape[2]
    core = lax.axis_index("run")
    me = lax.axis_index("shard")
    z = me // 2
    y = me % 2
    orders = visit_order(planes)

    def order_of(s):
        d = jnp.int32(0)
        for a in range(planes):
            for b in range(planes):
                hit = jnp.where(z == a, 1, 0) * jnp.where(s == b, 1, 0)
                d = d + hit * orders[a][b]
        return d

    to_core = {"run": 1 - core}
    to_y = {"shard": z * 2 + 1 - y}
    to_up = {"shard": jnp.minimum(me + 2, n - 1)}
    to_dn = {"shard": jnp.maximum(me - 2, 0)}
    above = z < planes - 1
    below = z > 0

    def load(r):
        return pltpu.make_async_copy(x_hbm.at[r], x.at[r], in_sem.at[r])

    load_cot = pltpu.make_async_copy(cot_hbm, cot, in_sem.at[2])
    load_w = pltpu.make_async_copy(w_hbm, w4.at[pl.ds(0, 2)], in_sem.at[3])
    load_side = pltpu.make_async_copy(side_hbm, side4.at[pl.ds(0, 2)], in_sem.at[4])
    own_f = pltpu.make_async_copy(f_hbm, f_out.at[pl.ds(0, 2)], own_sem.at[0])
    own_s = pltpu.make_async_copy(s_hbm, s_out.at[pl.ds(0, 2)], own_sem.at[1])

    load(0).start()
    load_cot.start()
    load_w.start()
    load_side.start()
    load(1).start()

    barrier = pltpu.get_barrier_semaphore()
    pl.semaphore_signal(barrier, inc=1, device_id=to_core, device_id_type=MESH)
    pl.semaphore_signal(barrier, inc=1, device_id=to_y, device_id_type=MESH)

    @pl.when(above)
    def _():
        pl.semaphore_signal(barrier, inc=1, device_id=to_up, device_id_type=MESH)

    @pl.when(below)
    def _():
        pl.semaphore_signal(barrier, inc=1, device_id=to_dn, device_id_type=MESH)

    pl.semaphore_wait(barrier, 2 + jnp.where(above, 1, 0) + jnp.where(below, 1, 0))

    def remote(src, dst, send, recv, where):
        return pltpu.make_async_remote_copy(
            src_ref=src, dst_ref=dst, send_sem=send, recv_sem=recv, device_id=where, device_id_type=MESH
        )

    far = pl.ds(2, 2)
    state = [
        remote(w_hbm, w4.at[far], st_send.at[0], st_recv.at[0], to_core),
        remote(side_hbm, side4.at[far], st_send.at[1], st_recv.at[1], to_core),
        remote(f_hbm, f_out.at[far], st_send.at[2], st_recv.at[2], to_core),
        remote(s_hbm, s_out.at[far], st_send.at[3], st_recv.at[3], to_core),
    ]
    state[0].start()
    state[1].start()

    def y_copy(k):
        return remote(ysend.at[k], yrecv.at[k], y_send.at[k], y_recv.at[k], to_y)

    def columns(shard):
        return pl.ds(pl.multiple_of(shard * rows, rows), rows)

    def share(r, shard):
        return lax.dot_general(
            x[r, :, columns(shard)], cot[r], (((0,), (0,)), ((), ())), preferred_element_type=F32
        )

    def scale_tokens(r):
        def body(i, carry):
            at = pl.ds(pl.multiple_of(i * 16, 16), 16)
            v = x[r, at, :].astype(F32)
            q = lax.rsqrt(jnp.sum(v * v, axis=-1, keepdims=True) * (1.0 / features) + 1e-05)
            inv[r, at, :] = q
            cot[r, at, :] = (cot[r, at, :].astype(F32) * q).astype(BF16)
            return carry

        lax.fori_loop(0, tokens // 16, body, 0)

    def send_y(k):
        d = order_of(k // 2)
        ysend[k] = share(k % 2, d * 2 + 1 - y).astype(BF16)
        y_copy(k).start()

    def z_copy(k):
        d = order_of(k // 2)
        r = k % 2
        up = d > z
        slot = jnp.where(d == z - 1, 2 * planes + r, d * 2 + r)
        to = jnp.where(up, jnp.minimum(z + 1, planes - 1), jnp.maximum(z - 1, 0)) * 2 + y
        return remote(yrecv.at[k], zrecv.at[slot], z_send.at[k], z_recv.at[slot], {"shard": to})

    def z_wait(slot):
        remote(zrecv.at[slot], zrecv.at[slot], z_send.at[0], z_recv.at[slot], to_y).wait_recv()

    def grad_copy(r):
        return pltpu.make_async_copy(tmp.at[r], grad_hbm.at[r], out_sem.at[r])

    def sum_step(k):
        s = k // 2
        r = k % 2
        d = order_of(s)
        total = share(r, d * 2 + y)
        y_copy(k).wait_recv()
        tmp[r] = total + yrecv[k].astype(F32)
        slot = d * 2 + r
        from_below = jnp.logical_and(d >= z, below)
        from_above = jnp.logical_and(d < z, above)

        @pl.when(jnp.logical_or(from_below, from_above))
        def _():
            z_wait(slot)
            tmp[r] += zrecv[slot].astype(F32)

        @pl.when(s < planes - 1)
        def _():
            yrecv[k] = tmp[r].astype(BF16)
            z_copy(k).start()

        @pl.when(s == planes - 1)
        def _():
            @pl.when(above)
            def _():
                z_wait(2 * planes + r)
                tmp[r] += zrecv[2 * planes + r].astype(F32)

            grad_copy(r).start()

    def ag_copy(shard, sem, to):
        return remote(gmine.at[shard], gmine.at[shard], sem, ag_recv.at[shard], to)

    def core_copy(shard):
        return remote(gmine.at[shard], gother.at[shard], co_send.at[shard], co_recv.at[shard], to_core)

    def hand_on(shard, go_up, go_dn):
        @pl.when(go_up)
        def _():
            ag_copy(shard, up_send.at[shard], to_up).start()

        @pl.when(go_dn)
        def _():
            ag_copy(shard, dn_send.at[shard], to_dn).start()

        core_copy(shard).start()

    def sources(i):
        h = i // 2
        o = i % 2
        yy = jnp.where(o == 0, y, 1 - y)
        lower = jnp.maximum(z - h, 0) * 2 + yy
        upper = jnp.minimum(z + h, planes - 1) * 2 + yy
        has_upper = jnp.logical_and(h > 0, z + h < planes)
        return h, lower, z - h >= 0, upper, has_upper

    def gather_step(i):
        h, lower, has_lower, upper, has_upper = sources(i)

        @pl.when(has_lower)
        def _():
            ag_copy(lower, ay_send.at[0], to_y).wait_recv()
            hand_on(lower, above, jnp.logical_and(h == 0, below))

        @pl.when(has_upper)
        def _():
            ag_copy(upper, ay_send.at[0], to_y).wait_recv()
            hand_on(upper, False, below)

    def use(shard):
        core_copy(shard).wait_recv()

        def body(r, carry):
            keep = mine_ref[pl.ds(r, 1), :]
            w = gmine[shard].astype(F32) * keep + gother[shard].astype(F32) * (1.0 - keep)
            acc[r] += jnp.dot(x[r, :, columns(shard)], w.astype(BF16), preferred_element_type=F32)
            return carry

        lax.fori_loop(0, runs, body, 0)

    def use_step(i):
        _, lower, has_lower, upper, has_upper = sources(i)

        @pl.when(has_lower)
        def _():
            use(lower)

        @pl.when(has_upper)
        def _():
            use(upper)

    load_cot.wait()
    load(0).wait()
    scale_tokens(0)
    send_y(0)

    load_w.wait()
    load_side.wait()
    state[0].wait_recv()
    state[1].wait_recv()
    pick = pick_ref[0]
    gain = side4[pick, 0:rows, :]
    for q in range(width // 128):
        cut = slice(q * 128, (q + 1) * 128)
        gmine[me, :, cut] = (w4[pick, :, cut] * gain).astype(BF16)
    ag_copy(me, ay_send.at[0], to_y).start()
    hand_on(me, above, below)
    state[2].start()
    state[3].start()
    own_f.start()
    own_s.start()
    put_w = pltpu.make_async_copy(w4, w_out, own_sem.at[2])
    put_side = pltpu.make_async_copy(side4, side_out, own_sem.at[3])
    put_w.start()
    put_side.start()

    load(1).wait()
    scale_tokens(1)
    acc[...] = jnp.zeros_like(acc)

    def step(t, carry):
        @pl.when(t < steps)
        def _():
            send_y(t)

        k = t - AHEAD

        @pl.when(k >= 0)
        def _():
            sum_step(k)

            @pl.when(k + 1 < steps)
            def _():
                gather_step(k + 1)

            use_step(k)

        return carry

    lax.fori_loop(1, steps + AHEAD, step, 0)

    def finish(i, carry):
        r = i // (tokens // 16)
        at = pl.ds(pl.multiple_of((i % (tokens // 16)) * 16, 16), 16)
        cot[r, at, :] = (acc[r, at, :] * (inv[r, at, :] * features ** (-0.5))).astype(BF16)
        return carry

    lax.fori_loop(0, runs * (tokens // 16), finish, 0)
    put_keys = pltpu.make_async_copy(cot, keys_hbm, out_sem.at[2])
    put_keys.start()

    def drain(k, carry):
        y_copy(k).wait_send()

        @pl.when(k < steps - 2)
        def _():
            z_copy(k).wait_send()

        return carry

    lax.fori_loop(0, steps, drain, 0)
    ag_copy(me, ay_send.at[0], to_y).wait_send()

    def drain_gather(shard, carry):
        core_copy(shard).wait_send()

        @pl.when(jnp.logical_and(above, shard // 2 <= z))
        def _():
            ag_copy(shard, up_send.at[shard], to_up).wait_send()

        @pl.when(jnp.logical_and(below, shard // 2 >= z))
        def _():
            ag_copy(shard, dn_send.at[shard], to_dn).wait_send()

        return carry

    lax.fori_loop(0, n, drain_gather, 0)
    for copy in state:
        copy.wait_send()
    state[2].wait_recv()
    state[3].wait_recv()
    own_f.wait()
    own_s.wait()
    put_w.wait()
    put_side.wait()
    put_keys.wait()
    grad_copy(0).wait()
    grad_copy(1).wait()


def exchange(n, pick, mine, inputs, cotangent, weight, first, second, side):
    runs, tokens, features = inputs.shape
    rows, width = weight.shape[1:]
    steps = n
    dma = pltpu.SemaphoreType.DMA
    any_spec = pl.BlockSpec(memory_space=pl.ANY)
    four = jax.ShapeDtypeStruct((2 * runs, rows, width), F32)
    return pl.pallas_call(
        functools.partial(exchange_kernel, n),
        out_shape=(
            jax.ShapeDtypeStruct((runs, tokens, width), BF16),
            jax.ShapeDtypeStruct((runs, rows, width), F32),
            four,
            four,
            four,
            jax.ShapeDtypeStruct((2 * runs,) + side.shape[1:], F32),
        ),
        in_specs=[
            pl.BlockSpec(memory_space=pltpu.SMEM),
            pl.BlockSpec(memory_space=pltpu.VMEM),
        ]
        + [any_spec] * 6,
        out_specs=(any_spec,) * 6,
        scratch_shapes=[
            pltpu.VMEM((runs, tokens, features), BF16),
            pltpu.VMEM((runs, tokens, width), BF16),
            pltpu.VMEM((runs, tokens, 1), F32),
            pltpu.VMEM((2 * runs, rows, width), F32),
            pltpu.VMEM((2 * runs,) + side.shape[1:], F32),
            pltpu.VMEM((steps, rows, width), BF16),
            pltpu.VMEM((steps, rows, width), BF16),
            pltpu.VMEM((steps + 2, rows, width), BF16),
            pltpu.VMEM((n, rows, width), BF16),
            pltpu.VMEM((n, rows, width), BF16),
            pltpu.VMEM((runs, tokens, width), F32),
            pltpu.VMEM((runs, rows, width), F32),
            dma((5,)),
            dma((4,)),
            dma((3,)),
            dma((4,)),
            dma((4,)),
            dma((steps,)),
            dma((steps,)),
            dma((steps,)),
            dma((steps + 2,)),
            dma((1,)),
            dma((n,)),
            dma((n,)),
            dma((n,)),
            dma((n,)),
            dma((n,)),
        ],
        compiler_params=pltpu.CompilerParams(
            collective_id=0, has_side_effects=True, vmem_limit_bytes=60 * 1024 * 1024
        ),
        cost_estimate=pl.CostEstimate(
            flops=4 * runs * tokens * features * width, bytes_accessed=40_000_000, transcendentals=0
        ),
        name="exchange",
    )(pick, mine, inputs, cotangent, weight, first, second, side)


def update_kernel(source_ref, factor_ref, grad, w, f, s, side, new_w, new_f, new_s, hyper, *, rows, scale):
    r = pl.program_id(0)
    j = pl.program_id(1)
    height, width = grad.shape[1:]
    tile = lambda v: jnp.concatenate([v] * (width // 128), axis=1)
    gain = side[0, pl.ds(pl.multiple_of(j * height, 8), height), :] * scale
    rate = side[0, rows : rows + 1, :] * factor_ref[r, 0]
    beta = 1.0 - (1.0 - side[0, rows + 1 : rows + 2, :]) * factor_ref[r, 1]

    @pl.when(j == 0)
    def _():
        at = lax.broadcasted_iota(jnp.int32, (1, 2), 1)
        hyper[pl.ds(r, 1), :] = jnp.where(at == 0, rate[:, :2], beta[:, :2])

    rate, beta = tile(rate), tile(beta)
    g = grad[0] * tile(gain)
    first = beta * f[0] + (1.0 - beta) * g
    second = 0.95 * s[0] + 0.05 * g * g
    new_f[0] = first
    new_s[0] = second
    new_w[0] = w[0] - rate * first / (jnp.sqrt(second) + 1e-08)


def update(source, factor, grad, w4, f4, s4, side4, scale):
    runs, rows, width = grad.shape
    height = min(256, rows)
    own = pl.BlockSpec((1, height, width), lambda r, j, src: (r, j, 0))
    taken = pl.BlockSpec((1, height, width), lambda r, j, src: (src[r], j, 0))
    out = jax.ShapeDtypeStruct(grad.shape, F32)
    return pl.pallas_call(
        functools.partial(update_kernel, rows=rows, scale=scale),
        out_shape=(out, out, out, jax.ShapeDtypeStruct((runs, 2), F32)),
        grid_spec=pltpu.PrefetchScalarGridSpec(
            num_scalar_prefetch=1,
            grid=(runs, rows // height),
            in_specs=[
                pl.BlockSpec(memory_space=pltpu.SMEM),
                own,
                taken,
                taken,
                taken,
                pl.BlockSpec((1,) + side4.shape[1:], lambda r, j, src: (src[r], 0, 0)),
            ],
            out_specs=(own, own, own, pl.BlockSpec((runs, 2), lambda r, j, src: (0, 0))),
        ),
        compiler_params=pltpu.CompilerParams(vmem_limit_bytes=40 * 1024 * 1024),
        name="update",
    )(source, factor, grad, w4, f4, s4, side4)


def per_device(
    n,
    weight,
    first_moment,
    second_moment,
    norm_gain,
    learning_rate,
    momentum,
    inputs,
    cotangent,
    winner,
    perturb,
):
    runs, rows, width = weight.shape
    features = inputs.shape[2]
    core = lax.axis_index("run")
    shard = lax.axis_index("shard")
    offset = core * runs
    everyone = jnp.arange(winner.shape[0], dtype=jnp.int32)
    mine = offset + jnp.arange(runs, dtype=jnp.int32)
    named = winner == everyone
    low = jnp.min(jnp.where(named, everyone, winner.shape[0]))
    high = jnp.max(jnp.where(named, everyone, -1))
    chosen = jnp.where(core == 0, low, high)

    def place(run):
        return jnp.where(run // runs == core, run % runs, runs + run % runs).astype(jnp.int32)

    source = lax.dynamic_slice(winner, (offset,), (runs,))
    codes = lax.dynamic_slice(perturb, (offset, jnp.int32(0)), (runs, 2))
    factor = jnp.where(codes == 0, F32(0.8), F32(1.25))
    factor = jnp.where((source != mine)[:, None], factor, F32(1.0))
    gain = lax.dynamic_slice(norm_gain, (jnp.int32(0), shard * rows), (runs, rows))
    side = jnp.concatenate(
        [gain, learning_rate[:, None], momentum[:, None], jnp.zeros((runs, 6), F32)], axis=1
    )
    side = jnp.broadcast_to(side[:, :, None], side.shape + (128,))
    same = jnp.broadcast_to((source == chosen).astype(F32)[:, None], (runs, width))
    keys, grad, w4, f4, s4, side4 = exchange(
        n, place(chosen)[None], same, inputs, cotangent, weight, first_moment, second_moment, side
    )
    new_weight, new_first, new_second, new_hyper = update(
        place(source), factor, grad, w4, f4, s4, side4, features ** (-0.5)
    )
    return (keys, new_weight, new_first, new_second, new_hyper)


def solution(mesh):
    rows = P(("group", "run"), "shard", None)
    placed = (
        rows,
        rows,
        rows,
        P(("group", "run"), None),
        P(("group", "run")),
        P(("group", "run")),
        rows,
        rows,
        P("group"),
        P("group", None),
    )
    return jax.shard_map(
        functools.partial(per_device, mesh.shape["shard"]),
        mesh=mesh,
        in_specs=placed,
        out_specs=(rows, rows, rows, rows, P(("group", "run"), None)),
        check_vma=False,
    )
```

```python
import functools

import jax
import jax.numpy as jnp
from jax import lax
from jax.experimental import pallas as pl
from jax.experimental.pallas import tpu as pltpu
from jax.sharding import PartitionSpec as P

MESH = pl.DeviceIdType.MESH
F32 = jnp.float32
BF16 = jnp.bfloat16
AHEAD = 3


def visit_order(planes):
    return [sorted(range(planes), key=lambda d: (-abs(d - z), -d)) for z in range(planes)]


def exchange_kernel(
    n,
    pick_ref,
    mine_ref,
    x_hbm,
    cot_hbm,
    w_hbm,
    f_hbm,
    s_hbm,
    side_hbm,
    keys_hbm,
    grad_hbm,
    w_out,
    f_out,
    s_out,
    side_out,
    x,
    cot,
    inv,
    w4,
    side4,
    ysend,
    yrecv,
    zrecv,
    gmine,
    gother,
    acc,
    tmp,
    in_sem,
    own_sem,
    out_sem,
    st_send,
    st_recv,
    y_send,
    y_recv,
    z_send,
    z_recv,
    ay_send,
    up_send,
    dn_send,
    ag_recv,
    co_send,
    co_recv,
):
    planes = n // 2
    steps = 2 * planes
    runs, tokens, features = x.shape
    rows = features // n
    width = cot.shape[2]
    core = lax.axis_index("run")
    me = lax.axis_index("shard")
    z = me // 2
    y = me % 2
    orders = visit_order(planes)

    def order_of(s):
        d = jnp.int32(0)
        for a in range(planes):
            for b in range(planes):
                hit = jnp.where(z == a, 1, 0) * jnp.where(s == b, 1, 0)
                d = d + hit * orders[a][b]
        return d

    to_core = {"run": 1 - core}
    to_y = {"shard": z * 2 + 1 - y}
    to_up = {"shard": jnp.minimum(me + 2, n - 1)}
    to_dn = {"shard": jnp.maximum(me - 2, 0)}
    above = z < planes - 1
    below = z > 0

    def load(r):
        return pltpu.make_async_copy(x_hbm.at[r], x.at[r], in_sem.at[r])

    load_cot = pltpu.make_async_copy(cot_hbm, cot, in_sem.at[2])
    load_w = pltpu.make_async_copy(w_hbm, w4.at[pl.ds(0, 2)], in_sem.at[3])
    load_side = pltpu.make_async_copy(side_hbm, side4.at[pl.ds(0, 2)], in_sem.at[4])
    own_f = pltpu.make_async_copy(f_hbm, f_out.at[pl.ds(0, 2)], own_sem.at[0])
    own_s = pltpu.make_async_copy(s_hbm, s_out.at[pl.ds(0, 2)], own_sem.at[1])

    load(0).start()
    load_cot.start()
    load_w.start()
    load_side.start()

    barrier = pltpu.get_barrier_semaphore()
    pl.semaphore_signal(barrier, inc=1, device_id=to_core, device_id_type=MESH)
    pl.semaphore_signal(barrier, inc=1, device_id=to_y, device_id_type=MESH)

    @pl.when(above)
    def _():
        pl.semaphore_signal(barrier, inc=1, device_id=to_up, device_id_type=MESH)

    @pl.when(below)
    def _():
        pl.semaphore_signal(barrier, inc=1, device_id=to_dn, device_id_type=MESH)

    pl.semaphore_wait(barrier, 2 + jnp.where(above, 1, 0) + jnp.where(below, 1, 0))

    def remote(src, dst, send, recv, where):
        return pltpu.make_async_remote_copy(
            src_ref=src, dst_ref=dst, send_sem=send, recv_sem=recv, device_id=where, device_id_type=MESH
        )

    far = pl.ds(2, 2)
    state = [
        remote(w_hbm, w4.at[far], st_send.at[0], st_recv.at[0], to_core),
        remote(side_hbm, side4.at[far], st_send.at[1], st_recv.at[1], to_core),
        remote(f_hbm, f_out.at[far], st_send.at[2], st_recv.at[2], to_core),
        remote(s_hbm, s_out.at[far], st_send.at[3], st_recv.at[3], to_core),
    ]
    state[0].start()
    state[1].start()

    def y_copy(k):
        return remote(ysend.at[k], yrecv.at[k], y_send.at[k], y_recv.at[k], to_y)

    def columns(shard):
        return pl.ds(pl.multiple_of(shard * rows, rows), rows)

    def share(r, shard):
        return lax.dot_general(
            x[r, :, columns(shard)], cot[r], (((0,), (0,)), ((), ())), preferred_element_type=F32
        )

    def scale_tokens(r):
        def body(i, carry):
            at = pl.ds(pl.multiple_of(i * 16, 16), 16)
            v = x[r, at, :].astype(F32)
            q = lax.rsqrt(jnp.sum(v * v, axis=-1, keepdims=True) * (1.0 / features) + 1e-05)
            inv[r, at, :] = q
            cot[r, at, :] = (cot[r, at, :].astype(F32) * q).astype(BF16)
            return carry

        lax.fori_loop(0, tokens // 16, body, 0, unroll=4)

    def send_y(k):
        d = order_of(k // 2)
        ysend[k] = share(k % 2, d * 2 + 1 - y).astype(BF16)
        y_copy(k).start()

    def z_copy(k):
        d = order_of(k // 2)
        r = k % 2
        up = d > z
        slot = jnp.where(d == z - 1, 2 * planes + r, d * 2 + r)
        to = jnp.where(up, jnp.minimum(z + 1, planes - 1), jnp.maximum(z - 1, 0)) * 2 + y
        return remote(yrecv.at[k], zrecv.at[slot], z_send.at[k], z_recv.at[slot], {"shard": to})

    def z_wait(slot):
        remote(zrecv.at[slot], zrecv.at[slot], z_send.at[0], z_recv.at[slot], to_y).wait_recv()

    def grad_copy(r):
        return pltpu.make_async_copy(tmp.at[r], grad_hbm.at[r], out_sem.at[r])

    def sum_step(k):
        s = k // 2
        r = k % 2
        d = order_of(s)
        total = share(r, d * 2 + y)
        y_copy(k).wait_recv()
        tmp[r] = total + yrecv[k].astype(F32)
        slot = d * 2 + r
        from_below = jnp.logical_and(d >= z, below)
        from_above = jnp.logical_and(d < z, above)

        @pl.when(jnp.logical_or(from_below, from_above))
        def _():
            z_wait(slot)
            tmp[r] += zrecv[slot].astype(F32)

        @pl.when(s < planes - 1)
        def _():
            yrecv[k] = tmp[r].astype(BF16)
            z_copy(k).start()

        @pl.when(s == planes - 1)
        def _():
            @pl.when(above)
            def _():
                z_wait(2 * planes + r)
                tmp[r] += zrecv[2 * planes + r].astype(F32)

            grad_copy(r).start()

    def ag_copy(shard, sem, to):
        return remote(gmine.at[shard], gmine.at[shard], sem, ag_recv.at[shard], to)

    def core_copy(shard):
        return remote(gmine.at[shard], gother.at[shard], co_send.at[shard], co_recv.at[shard], to_core)

    def hand_on(shard, go_up, go_dn):
        @pl.when(go_up)
        def _():
            ag_copy(shard, up_send.at[shard], to_up).start()

        @pl.when(go_dn)
        def _():
            ag_copy(shard, dn_send.at[shard], to_dn).start()

        core_copy(shard).start()

    def sources(i):
        h = i // 2
        o = i % 2
        yy = jnp.where(o == 0, y, 1 - y)
        lower = jnp.maximum(z - h, 0) * 2 + yy
        upper = jnp.minimum(z + h, planes - 1) * 2 + yy
        has_upper = jnp.logical_and(h > 0, z + h < planes)
        return h, lower, z - h >= 0, upper, has_upper

    def gather_step(i):
        h, lower, has_lower, upper, has_upper = sources(i)

        @pl.when(has_lower)
        def _():
            ag_copy(lower, ay_send.at[0], to_y).wait_recv()
            hand_on(lower, above, jnp.logical_and(h == 0, below))

        @pl.when(has_upper)
        def _():
            ag_copy(upper, ay_send.at[0], to_y).wait_recv()
            hand_on(upper, False, below)

    def use(shard):
        core_copy(shard).wait_recv()

        def body(r, carry):
            keep = mine_ref[pl.ds(r, 1), :]
            w = gmine[shard].astype(F32) * keep + gother[shard].astype(F32) * (1.0 - keep)
            acc[r] += jnp.dot(x[r, :, columns(shard)], w.astype(BF16), preferred_element_type=F32)
            return carry

        lax.fori_loop(0, runs, body, 0)

    def use_step(i):
        _, lower, has_lower, upper, has_upper = sources(i)

        @pl.when(has_lower)
        def _():
            use(lower)

        @pl.when(has_upper)
        def _():
            use(upper)

    load_cot.wait()
    load(0).wait()
    load(1).start()
    scale_tokens(0)
    send_y(0)

    load_w.wait()
    load_side.wait()
    state[0].wait_recv()
    state[1].wait_recv()
    pick = pick_ref[0]
    gain = side4[pick, 0:rows, :]
    for q in range(width // 128):
        cut = slice(q * 128, (q + 1) * 128)
        gmine[me, :, cut] = (w4[pick, :, cut] * gain).astype(BF16)
    ag_copy(me, ay_send.at[0], to_y).start()
    hand_on(me, above, below)
    state[2].start()
    state[3].start()
    own_f.start()
    own_s.start()
    put_w = pltpu.make_async_copy(w4, w_out, own_sem.at[2])
    put_side = pltpu.make_async_copy(side4, side_out, own_sem.at[3])
    put_w.start()
    put_side.start()

    load(1).wait()
    scale_tokens(1)
    acc[...] = jnp.zeros_like(acc)

    def step(t, carry):
        @pl.when(t < steps)
        def _():
            send_y(t)

        k = t - AHEAD

        @pl.when(k >= 0)
        def _():
            sum_step(k)

            @pl.when(k + 1 < steps)
            def _():
                gather_step(k + 1)

            use_step(k)

        return carry

    lax.fori_loop(1, steps + AHEAD, step, 0)

    def finish(i, carry):
        r = i // (tokens // 16)
        at = pl.ds(pl.multiple_of((i % (tokens // 16)) * 16, 16), 16)
        cot[r, at, :] = (acc[r, at, :] * (inv[r, at, :] * features ** (-0.5))).astype(BF16)
        return carry

    lax.fori_loop(0, runs * (tokens // 16), finish, 0, unroll=4)
    put_keys = pltpu.make_async_copy(cot, keys_hbm, out_sem.at[2])
    put_keys.start()

    def drain(k, carry):
        y_copy(k).wait_send()

        @pl.when(k < steps - 2)
        def _():
            z_copy(k).wait_send()

        return carry

    lax.fori_loop(0, steps, drain, 0)
    ag_copy(me, ay_send.at[0], to_y).wait_send()

    def drain_gather(shard, carry):
        core_copy(shard).wait_send()

        @pl.when(jnp.logical_and(above, shard // 2 <= z))
        def _():
            ag_copy(shard, up_send.at[shard], to_up).wait_send()

        @pl.when(jnp.logical_and(below, shard // 2 >= z))
        def _():
            ag_copy(shard, dn_send.at[shard], to_dn).wait_send()

        return carry

    lax.fori_loop(0, n, drain_gather, 0)
    for copy in state:
        copy.wait_send()
    state[2].wait_recv()
    state[3].wait_recv()
    own_f.wait()
    own_s.wait()
    put_w.wait()
    put_side.wait()
    put_keys.wait()
    grad_copy(0).wait()
    grad_copy(1).wait()


def exchange(n, pick, mine, inputs, cotangent, weight, first, second, side):
    runs, tokens, features = inputs.shape
    rows, width = weight.shape[1:]
    steps = n
    dma = pltpu.SemaphoreType.DMA
    any_spec = pl.BlockSpec(memory_space=pl.ANY)
    four = jax.ShapeDtypeStruct((2 * runs, rows, width), F32)
    return pl.pallas_call(
        functools.partial(exchange_kernel, n),
        out_shape=(
            jax.ShapeDtypeStruct((runs, tokens, width), BF16),
            jax.ShapeDtypeStruct((runs, rows, width), F32),
            four,
            four,
            four,
            jax.ShapeDtypeStruct((2 * runs,) + side.shape[1:], F32),
        ),
        in_specs=[
            pl.BlockSpec(memory_space=pltpu.SMEM),
            pl.BlockSpec(memory_space=pltpu.VMEM),
        ]
        + [any_spec] * 6,
        out_specs=(any_spec,) * 6,
        scratch_shapes=[
            pltpu.VMEM((runs, tokens, features), BF16),
            pltpu.VMEM((runs, tokens, width), BF16),
            pltpu.VMEM((runs, tokens, 1), F32),
            pltpu.VMEM((2 * runs, rows, width), F32),
            pltpu.VMEM((2 * runs,) + side.shape[1:], F32),
            pltpu.VMEM((steps, rows, width), BF16),
            pltpu.VMEM((steps, rows, width), BF16),
            pltpu.VMEM((steps + 2, rows, width), BF16),
            pltpu.VMEM((n, rows, width), BF16),
            pltpu.VMEM((n, rows, width), BF16),
            pltpu.VMEM((runs, tokens, width), F32),
            pltpu.VMEM((runs, rows, width), F32),
            dma((5,)),
            dma((4,)),
            dma((3,)),
            dma((4,)),
            dma((4,)),
            dma((steps,)),
            dma((steps,)),
            dma((steps,)),
            dma((steps + 2,)),
            dma((1,)),
            dma((n,)),
            dma((n,)),
            dma((n,)),
            dma((n,)),
            dma((n,)),
        ],
        compiler_params=pltpu.CompilerParams(
            collective_id=0, has_side_effects=True, vmem_limit_bytes=60 * 1024 * 1024
        ),
        cost_estimate=pl.CostEstimate(
            flops=4 * runs * tokens * features * width, bytes_accessed=40_000_000, transcendentals=0
        ),
        name="exchange",
    )(pick, mine, inputs, cotangent, weight, first, second, side)


def update_kernel(source_ref, factor_ref, grad, w, f, s, side, new_w, new_f, new_s, hyper, *, rows, scale):
    r = pl.program_id(0)
    j = pl.program_id(1)
    height, width = grad.shape[1:]
    tile = lambda v: jnp.concatenate([v] * (width // 128), axis=1)
    gain = side[0, pl.ds(pl.multiple_of(j * height, 8), height), :] * scale
    rate = side[0, rows : rows + 1, :] * factor_ref[r, 0]
    beta = 1.0 - (1.0 - side[0, rows + 1 : rows + 2, :]) * factor_ref[r, 1]

    @pl.when(j == 0)
    def _():
        at = lax.broadcasted_iota(jnp.int32, (1, 2), 1)
        hyper[pl.ds(r, 1), :] = jnp.where(at == 0, rate[:, :2], beta[:, :2])

    rate, beta = tile(rate), tile(beta)
    g = grad[0] * tile(gain)
    first = beta * f[0] + (1.0 - beta) * g
    second = 0.95 * s[0] + 0.05 * g * g
    new_f[0] = first
    new_s[0] = second
    new_w[0] = w[0] - rate * first / (jnp.sqrt(second) + 1e-08)


def update(source, factor, grad, w4, f4, s4, side4, scale):
    runs, rows, width = grad.shape
    height = min(256, rows)
    own = pl.BlockSpec((1, height, width), lambda r, j, src: (r, j, 0))
    taken = pl.BlockSpec((1, height, width), lambda r, j, src: (src[r], j, 0))
    out = jax.ShapeDtypeStruct(grad.shape, F32)
    return pl.pallas_call(
        functools.partial(update_kernel, rows=rows, scale=scale),
        out_shape=(out, out, out, jax.ShapeDtypeStruct((runs, 2), F32)),
        grid_spec=pltpu.PrefetchScalarGridSpec(
            num_scalar_prefetch=1,
            grid=(runs, rows // height),
            in_specs=[
                pl.BlockSpec(memory_space=pltpu.SMEM),
                own,
                taken,
                taken,
                taken,
                pl.BlockSpec((1,) + side4.shape[1:], lambda r, j, src: (src[r], 0, 0)),
            ],
            out_specs=(own, own, own, pl.BlockSpec((runs, 2), lambda r, j, src: (0, 0))),
        ),
        compiler_params=pltpu.CompilerParams(vmem_limit_bytes=40 * 1024 * 1024),
        name="update",
    )(source, factor, grad, w4, f4, s4, side4)


def per_device(
    n,
    weight,
    first_moment,
    second_moment,
    norm_gain,
    learning_rate,
    momentum,
    inputs,
    cotangent,
    winner,
    perturb,
):
    runs, rows, width = weight.shape
    features = inputs.shape[2]
    core = lax.axis_index("run")
    shard = lax.axis_index("shard")
    offset = core * runs
    everyone = jnp.arange(winner.shape[0], dtype=jnp.int32)
    mine = offset + jnp.arange(runs, dtype=jnp.int32)
    named = winner == everyone
    low = jnp.min(jnp.where(named, everyone, winner.shape[0]))
    high = jnp.max(jnp.where(named, everyone, -1))
    chosen = jnp.where(core == 0, low, high)

    def place(run):
        return jnp.where(run // runs == core, run % runs, runs + run % runs).astype(jnp.int32)

    source = lax.dynamic_slice(winner, (offset,), (runs,))
    codes = lax.dynamic_slice(perturb, (offset, jnp.int32(0)), (runs, 2))
    factor = jnp.where(codes == 0, F32(0.8), F32(1.25))
    factor = jnp.where((source != mine)[:, None], factor, F32(1.0))
    gain = lax.dynamic_slice(norm_gain, (jnp.int32(0), shard * rows), (runs, rows))
    side = jnp.concatenate(
        [gain, learning_rate[:, None], momentum[:, None], jnp.zeros((runs, 6), F32)], axis=1
    )
    side = jnp.broadcast_to(side[:, :, None], side.shape + (128,))
    same = jnp.broadcast_to((source == chosen).astype(F32)[:, None], (runs, width))
    keys, grad, w4, f4, s4, side4 = exchange(
        n, place(chosen)[None], same, inputs, cotangent, weight, first_moment, second_moment, side
    )
    new_weight, new_first, new_second, new_hyper = update(
        place(source), factor, grad, w4, f4, s4, side4, features ** (-0.5)
    )
    return (keys, new_weight, new_first, new_second, new_hyper)


def solution(mesh):
    rows = P(("group", "run"), "shard", None)
    placed = (
        rows,
        rows,
        rows,
        P(("group", "run"), None),
        P(("group", "run")),
        P(("group", "run")),
        rows,
        rows,
        P("group"),
        P("group", None),
    )
    return jax.shard_map(
        functools.partial(per_device, mesh.shape["shard"]),
        mesh=mesh,
        in_specs=placed,
        out_specs=(rows, rows, rows, rows, P(("group", "run"), None)),
        check_vma=False,
    )
```
